32 devices in a mesh: layer: 8 (over y, x, core), tp: 4 (over z).
Axes of the slice: x: 2, y: 2, z: 4, core: 2. Of those that a mesh axis runs over, the one named last changes fastest.
Arguments:
- acts: bfloat16 [1024, 2048], P(('layer', 'tp')), may hold values from -12 to 12, as said below
- fresh: bfloat16 [2, 128, 2048], P(None, 'tp'), may hold values from -12 to 12, as said below
- norm_first: float32 [4, 2048], replicated, may hold values from 0.5 to 1.5
- norm_second: float32 [4, 2048], replicated, may hold values from 0.5 to 1.5
- proj_qkv: bfloat16 [32, 2048, 192], P(('layer', 'tp')), may hold values from -1 to 1
- proj_out: bfloat16 [2048, 2048], P(('layer', 'tp')), may hold values from -0.25 to 0.25
- proj_gate_up: bfloat16 [2048, 2, 8192], P(None, None, ('layer', 'tp')), may hold values from -0.125 to 0.125
- proj_down: bfloat16 [8192, 2048], P(('layer', 'tp')), may hold values from -0.125 to 0.125
- memory_state: float32 [32, 64, 64], P(('layer', 'tp')), may hold values from -768 to 768
- memory_norm: float32 [32, 64], P(('layer', 'tp')), may hold values from 16 to 256
- bias_gate: float32 [32], P(('layer', 'tp')), may hold values from -3 to 3
Outputs:
- first_out: bfloat16 [1024, 2048], P(('layer', 'tp'))
- second_out: bfloat16 [1024, 2048], P(('layer', 'tp'))
- memory_after: float32 [32, 64, 64], P(('layer', 'tp'))
- norm_after: float32 [32, 64], P(('layer', 'tp'))
The draws below stay inside these ranges and needn't reach their ends.
Inputs may be any that keep to these rules, and one draw needn't show every extreme that they name: `acts`: activation rows. `fresh`: activation rows.
All inputs are finite; a program needn't handle non-finite values.
Results may differ from the reference program's by a relative error of at most 0.025.
Values may be sent and summed in bfloat16 or wider, within the bound.
A program may use at most 64 MiB of HBM per device.

```python
import math
import jax
import jax.numpy as jnp
from jax import lax

D = 2048
DH = 64
HEADS_DEV = 1
FF_DEV = 256
SEG = 256
HEADS = 8
FF = 2048
LAYERS = 4


def stream_draw(key, leading):
    base_key = jax.random.fold_in(key, 0)
    values = jax.random.normal(base_key, leading + (D,), jnp.float32)
    return jnp.clip(values, -12.0, 12.0)


def draw_acts(key, part):
    return stream_draw(key, (LAYERS * SEG,)).astype(jnp.bfloat16)


def draw_fresh(key, part):
    return stream_draw(key, (2, SEG // 2)).astype(jnp.bfloat16)


def draw_proj_qkv(key, part):
    key_one = jax.random.fold_in(key, 0)
    values = jax.random.normal(key_one, (LAYERS * HEADS, D, 3 * DH), jnp.float32) * D ** (-0.5)
    return jnp.clip(values, -1.0, 1.0).astype(jnp.bfloat16)


def shard_levels(rng, shape, cuts, smallest, top_value):
    gain = 1.0
    for axis_at, blocks in cuts:
        steps = jax.random.uniform(jax.random.fold_in(jax.random.fold_in(rng, 6), axis_at), (blocks,), jnp.float32, smallest / len(cuts), top_value / len(cuts))
        gain = gain * jnp.repeat(jnp.exp(steps), shape[axis_at] // blocks).reshape((-1,) + (1,) * (len(shape) - 1 - axis_at))
    return gain


def centred(own_key, extent, deviation, reach, cuts=(), dtype=jnp.bfloat16):
    values = jax.random.normal(own_key, extent, jnp.float32) * deviation
    if len(cuts) > 0:
        values = shard_levels(own_key, extent, cuts, -0.22, 0.18) * values
    return jnp.clip(values, min=-reach, max=reach).astype(dtype)


def setup_inputs(seed: int = 0) -> dict:
    key_of = jax.random.split(jax.random.key(seed), 12)
    acts = draw_acts(jax.random.fold_in(key_of[11], 71), 0)
    fresh = draw_fresh(jax.random.fold_in(key_of[11], 71), 0)
    norm_first = jnp.clip(1.0 + 0.1 * jax.random.normal(key_of[2], (LAYERS, D), jnp.float32), 0.5, 1.5)
    norm_second = jnp.clip(1.0 + 0.1 * jax.random.normal(key_of[3], (LAYERS, D), jnp.float32), 0.5, 1.5)
    proj_qkv = draw_proj_qkv(jax.random.fold_in(key_of[11], 71), 0)
    proj_out = centred(key_of[5], (LAYERS * HEADS * DH, D), (HEADS * DH) ** -0.5, 0.25, ((0, 32),))
    proj_gate_up = centred(key_of[6], (D, 2, LAYERS * FF), D ** -0.5, 0.125, ((2, 32),))
    proj_down = centred(key_of[7], (LAYERS * FF, D), FF ** -0.5, 0.125, ((0, 32),))
    memory_state = centred(key_of[8], (LAYERS * HEADS, DH, DH), 128.0, 768.0, ((0, 32),), jnp.float32)
    memory_norm = jnp.clip(jnp.exp(math.log(256.0) - 2.7725887 * jax.random.uniform(key_of[9], (LAYERS * HEADS, DH), jnp.float32) ** shard_levels(key_of[9], (LAYERS * HEADS, DH), ((0, 32),), -0.2, 0.2)), 16.0, 256.0)
    bias_gate = jnp.clip(jax.random.uniform(key_of[10], (LAYERS * HEADS,), jnp.float32, -3.0, 3.0) * shard_levels(key_of[10], (LAYERS * HEADS,), ((0, 32),), -0.4, 0.0), -3.0, 3.0)
    return {"acts": acts, "fresh": fresh, "norm_first": norm_first, "norm_second": norm_second, "proj_qkv": proj_qkv, "proj_out": proj_out, "proj_gate_up": proj_gate_up, "proj_down": proj_down, "memory_state": memory_state, "memory_norm": memory_norm, "bias_gate": bias_gate}


def rms_norm(values, weight):
    floats = values.astype(jnp.float32)
    scaled = floats * lax.rsqrt(lax.optimization_barrier(jnp.mean(floats * floats, axis=-1, keepdims=True)) + 1e-05)
    return (scaled * weight).astype(jnp.bfloat16)

def one_layer(stream, gain_one, gain_two, weight_qkv, weight_out, weight_gu, weight_down, memory, totals, logits):
    head_dim = memory.shape[-1]
    seg_len = stream.shape[0]
    width = weight_out.shape[1]
    normed = rms_norm(stream, gain_one)
    qkv = jnp.einsum('sd,hdc->shc', normed.astype(jnp.float32), weight_qkv.astype(jnp.float32)).astype(jnp.bfloat16)
    queries = qkv[..., :head_dim].astype(jnp.float32)
    keyed = qkv[..., head_dim:2 * head_dim].astype(jnp.float32)
    valued = qkv[..., 2 * head_dim:].astype(jnp.float32)
    scores = jnp.einsum('qhc,khc->hqk', queries, keyed) * head_dim ** (-0.5)
    positions = jnp.arange(seg_len)
    allowed = positions[:, None] >= positions[None, :]
    probs = jax.nn.softmax(jnp.where(allowed[None], scores, -jnp.inf), axis=-1).astype(jnp.bfloat16)
    direct = jnp.einsum('hqk,khc->qhc', probs.astype(jnp.float32), valued)
    lifted_q = jax.nn.elu(queries) + 1.0
    lifted_k = jax.nn.elu(keyed) + 1.0
    numer = jnp.einsum('qhc,hce->qhe', lifted_q, memory, precision=lax.Precision.HIGHEST)
    denom = jnp.einsum('qhc,hc->qh', lifted_q, totals, precision=lax.Precision.HIGHEST)[..., None]
    gate_open = jax.nn.sigmoid(logits)[None, :, None]
    blended = (gate_open * numer / denom + (1.0 - gate_open) * direct).astype(jnp.bfloat16)
    new_memory = memory + jnp.einsum('khc,khe->hce', lifted_k, valued, precision=lax.Precision.HIGHEST)
    new_totals = totals + lax.optimization_barrier(jnp.sum(lifted_k, axis=0))
    head_groups = HEADS // HEADS_DEV
    grouped = blended.reshape(seg_len, head_groups, -1).astype(jnp.float32)
    parts = jnp.einsum('snk,nkd->nsd', grouped, weight_out.reshape(head_groups, -1, width).astype(jnp.float32))
    rounded = lax.optimization_barrier(parts.astype(jnp.bfloat16))
    attn = lax.optimization_barrier(jnp.sum(rounded.astype(jnp.float32), axis=0))
    hidden_one = (stream.astype(jnp.float32) + attn).astype(jnp.bfloat16)
    normed_two = rms_norm(hidden_one, gain_two)
    gate_up = jnp.einsum('sd,dtf->stf', normed_two.astype(jnp.float32), weight_gu.astype(jnp.float32))
    hidden = (jax.nn.silu(gate_up[:, 0]) * gate_up[:, 1]).astype(jnp.bfloat16)
    unit_groups = FF // FF_DEV
    dparts = jnp.einsum('snf,nfd->nsd', hidden.reshape(seg_len, unit_groups, -1).astype(jnp.float32), weight_down.reshape(unit_groups, -1, width).astype(jnp.float32))
    drounded = lax.optimization_barrier(dparts.astype(jnp.bfloat16))
    ffn = lax.optimization_barrier(jnp.sum(drounded.astype(jnp.float32), axis=0))
    output = (hidden_one.astype(jnp.float32) + ffn).astype(jnp.bfloat16)
    return (output, new_memory, new_totals)

def reference(acts, fresh, norm_first, norm_second, proj_qkv, proj_out, proj_gate_up, proj_down, memory_state, memory_norm, bias_gate):
    acts_l = acts.reshape(LAYERS, SEG, D)
    fresh_rows = fresh.reshape(SEG, D)
    qkv_l = proj_qkv.reshape(LAYERS, HEADS, D, 3 * DH)
    out_l = proj_out.reshape(LAYERS, HEADS * DH, D)
    gu_l = jnp.transpose(proj_gate_up.reshape(D, 2, LAYERS, FF), (2, 0, 1, 3))
    down_l = proj_down.reshape(LAYERS, FF, D)
    memory_l = memory_state.reshape(LAYERS, HEADS, DH, DH)
    totals_l = memory_norm.reshape(LAYERS, HEADS, DH)
    bias_l = bias_gate.reshape(LAYERS, HEADS)

    def run_all(inputs, memory, totals):
        return lax.map(lambda items: one_layer(*items), (inputs, norm_first, norm_second, qkv_l, out_l, gu_l, down_l, memory, totals, bias_l))
    first_out, memory_one, totals_one = run_all(acts_l, memory_l, totals_l)
    incoming = jnp.concatenate([fresh_rows[None], first_out[:-1]], axis=0)
    second_out, memory_two, totals_two = run_all(incoming, memory_one, totals_one)
    return (first_out.reshape(LAYERS * SEG, D), second_out.reshape(LAYERS * SEG, D), memory_two.reshape(LAYERS * HEADS, DH, DH), totals_two.reshape(LAYERS * HEADS, DH))
```

```python
import functools

import jax
import jax.numpy as jnp
from jax import lax
from jax.experimental import pallas as pl
from jax.experimental.pallas import tpu as pltpu
from jax.sharding import PartitionSpec as P

MESH = pl.DeviceIdType.MESH
F32 = jnp.float32
BF16 = jnp.bfloat16
CHUNKS = 2


def flat(value):
    blocks, rows, columns = value.shape
    if rows % 16 == 0 or value.dtype == F32:
        return value.reshape(blocks * rows, columns)
    return value.astype(F32).reshape(blocks * rows, columns).astype(value.dtype)


def norm(values, gain):
    scaled = values * lax.rsqrt(jnp.mean(values * values, axis=-1, keepdims=True) + 1e-05)
    return (scaled * gain).astype(BF16)


def lifted(values):
    return jnp.maximum(values, 0.0) + jnp.exp(jnp.minimum(values, 0.0))


def kernel(
    n_layer,
    group,
    acts,
    fresh,
    gain_first,
    gain_second,
    w_qkv_hbm,
    w_out_hbm,
    w_gu_hbm,
    w_down_hbm,
    memory,
    totals,
    logit,
    first_out,
    second_out,
    memory_out,
    totals_out,
    w_qkv,
    w_out,
    w_gu,
    w_down,
    gathered,
    qkv,
    blended,
    hidden,
    given,
    taken,
    summed,
    arrived,
    stream,
    total,
    shifted,
    w_sem,
    ag_send,
    fw_send,
    ag_recv,
    x_send,
    x_recv,
    r_send,
    r_recv,
    sh_sem,
):
    place = lax.axis_index("layer")
    me = lax.axis_index("tp")
    half = lax.rem(place, 2)
    depth = lax.div(place, 2)
    base = half * group
    other_base = (1 - half) * group
    partner = (place + 1 - 2 * half, me)
    rows, width = acts.shape
    cols = width // CHUNKS
    head = memory.shape[-1]
    ff = w_down.shape[0]
    following = (lax.rem(place + 2, n_layer), me)
    previous = (lax.rem(place + n_layer - 2, n_layer), me)

    weights = [
        pltpu.make_async_copy(hbm, vmem, w_sem.at[k])
        for k, (hbm, vmem) in enumerate(
            [(w_qkv_hbm, w_qkv), (w_out_hbm, w_out), (w_gu_hbm, w_gu), (w_down_hbm, w_down)]
        )
    ]
    for copy in weights:
        copy.start()

    def peer(step):
        return lax.rem(me + step, group)

    barrier = pltpu.get_barrier_semaphore()
    for device in (partner, following, previous):
        pl.semaphore_signal(barrier, inc=1, device_id=device, device_id_type=MESH)

    def greet(step, _):
        pl.semaphore_signal(barrier, inc=1, device_id=(place, peer(step)), device_id_type=MESH)
        return 0

    lax.fori_loop(1, group, greet, 0)
    pl.semaphore_wait(barrier, 3 + group - 1)

    def block_copy(phase, slot, send_sem, device):
        return pltpu.make_async_remote_copy(
            src_ref=gathered.at[phase, slot],
            dst_ref=gathered.at[phase, slot],
            send_sem=send_sem,
            recv_sem=ag_recv.at[phase, slot],
            device_id=device,
            device_id_type=MESH,
        )

    def gather(phase, values, work):
        mine = base + me
        gathered[phase, mine] = values

        def send(step, _):
            target = peer(step)
            block_copy(phase, mine, ag_send.at[phase, target], (place, target)).start()
            return 0

        lax.fori_loop(1, group, send, 0)
        block_copy(phase, mine, ag_send.at[phase, me], partner).start()
        if phase < 2:
            weights[2 * phase].wait()
        work(mine)
        block_copy(phase, other_base + me, ag_send.at[phase, me], partner).wait_recv()
        work(other_base + me)

        def forward(step, _):
            source = peer(group - step)
            slot = base + source
            block_copy(phase, slot, ag_send.at[phase, me], partner).wait_recv()
            block_copy(phase, slot, fw_send.at[phase, source], partner).start()
            work(slot)
            return 0

        lax.fori_loop(1, group, forward, 0)

        def finish(step, _):
            slot = other_base + peer(group - step)
            block_copy(phase, slot, ag_send.at[phase, me], partner).wait_recv()
            work(slot)
            return 0

        lax.fori_loop(1, group, finish, 0)

    def exchange_copy(phase, chunk):
        part = pl.ds(chunk * cols, cols)
        return pltpu.make_async_remote_copy(
            src_ref=given.at[phase, :, :, part],
            dst_ref=taken.at[phase, :, :, part],
            send_sem=x_send.at[phase, chunk],
            recv_sem=x_recv.at[phase, chunk],
            device_id=partner,
            device_id_type=MESH,
        )

    def sum_copy(phase, chunk, target, source):
        part = pl.ds(chunk * cols, cols)
        return pltpu.make_async_remote_copy(
            src_ref=summed.at[phase, target, :, part],
            dst_ref=arrived.at[phase, source, :, part],
            send_sem=r_send.at[phase, chunk, target],
            recv_sem=r_recv.at[phase, chunk, source],
            device_id=(place, target),
            device_id_type=MESH,
        )

    def reduce(phase, local, weight, between):
        theirs = flat(local[pl.ds(other_base, group)])
        ours = flat(local[pl.ds(base, group)])
        for chunk in range(CHUNKS):
            part = slice(chunk * cols, (chunk + 1) * cols)
            term = jnp.dot(theirs, weight[:, part], preferred_element_type=F32)
            given[phase, :, :, part] = term.reshape(group, rows, cols).astype(BF16)
            exchange_copy(phase, chunk).start()
        for chunk in range(CHUNKS):
            part = slice(chunk * cols, (chunk + 1) * cols)
            term = jnp.dot(ours, weight[:, part], preferred_element_type=F32)
            exchange_copy(phase, chunk).wait_recv()
            term = term.reshape(group, rows, cols) + taken[phase, :, :, part].astype(F32)
            summed[phase, :, :, part] = term.astype(BF16)

            def send(step, _):
                sum_copy(phase, chunk, peer(step), me).start()
                return 0

            lax.fori_loop(1, group, send, 0)
        between()
        for chunk in range(CHUNKS):
            part = slice(chunk * cols, (chunk + 1) * cols)
            total[:, part] += summed[phase, me, :, part].astype(F32)

            def add(step, _):
                source = peer(group - step)
                sum_copy(phase, chunk, me, source).wait_recv()
                total[:, part] += arrived[phase, source, :, part].astype(F32)
                return 0

            lax.fori_loop(1, group, add, 0)

    def project(phase):
        def work(slot):
            qkv[slot] = jnp.dot(
                gathered[phase, slot], w_qkv[...], preferred_element_type=F32
            ).astype(BF16)

        return work

    def expand(phase):
        def work(slot):
            both = jnp.dot(gathered[phase, slot], w_gu[...], preferred_element_type=F32)
            gate = both[:, :ff]
            hidden[slot] = (gate / (1.0 + jnp.exp(-gate)) * both[:, ff:]).astype(BF16)

        return work

    def attend(memory_ref, totals_ref):
        all_rows = flat(qkv[...])
        seg = all_rows.shape[0]
        queries = all_rows[:, :head]
        keys = all_rows[:, head : 2 * head]
        values = all_rows[:, 2 * head :]
        scores = lax.dot_general(
            queries, keys, (((1,), (1,)), ((), ())), preferred_element_type=F32
        ) * head ** (-0.5)
        at_row = lax.broadcasted_iota(jnp.int32, (seg, seg), 0)
        at_col = lax.broadcasted_iota(jnp.int32, (seg, seg), 1)
        scores = jnp.where(at_row >= at_col, scores, -jnp.inf)
        powers = jnp.exp(scores - jnp.max(scores, axis=-1, keepdims=True))
        probs = (powers / jnp.sum(powers, axis=-1, keepdims=True)).astype(BF16)
        direct = jnp.dot(probs, values, preferred_element_type=F32)
        lifted_q = lifted(queries.astype(F32))
        numer = jnp.dot(
            lifted_q, memory_ref[...], preferred_element_type=F32, precision=lax.Precision.HIGHEST
        )
        denom = jnp.sum(lifted_q * totals_ref[...], axis=-1, keepdims=True)
        opened = 1.0 / (1.0 + jnp.exp(-logit[...]))
        mixed = opened * (numer / denom) + (1.0 - opened) * direct
        blended[...] = mixed.reshape(blended.shape).astype(BF16)

    def remember(memory_ref, totals_ref):
        all_rows = flat(qkv[...])
        lifted_k = lifted(all_rows[:, head : 2 * head].astype(F32))
        values = all_rows[:, 2 * head :].astype(F32)
        memory_out[...] = memory_ref[...] + lax.dot_general(
            lifted_k,
            values,
            (((0,), (0,)), ((), ())),
            preferred_element_type=F32,
            precision=lax.Precision.HIGHEST,
        )
        totals_out[...] = totals_ref[...] + jnp.sum(lifted_k, axis=0, keepdims=True)

    gain_one = gain_first[pl.ds(depth, 1), :]
    gain_two = gain_second[pl.ds(depth, 1), :]

    def layer(turn, memory_ref, totals_ref):
        first, second = 2 * turn, 2 * turn + 1
        start = stream[...].astype(F32)
        gather(first, norm(start, gain_one), project(first))
        total[...] = start
        attend(memory_ref, totals_ref)
        if turn == 0:
            weights[1].wait()
        reduce(first, blended, w_out, lambda: remember(memory_ref, totals_ref))
        middle = total[...].astype(BF16).astype(F32)
        gather_two = norm(middle, gain_two)
        total[...] = middle
        if turn == 0:
            gather(second, gather_two, expand(second))
            weights[3].wait()
        else:
            gather(second, gather_two, expand(second))
        reduce(second, hidden, w_down, lambda: None)

    stream[...] = acts[...]
    layer(0, memory, totals)
    first_out[...] = total[...].astype(BF16)
    relay = pltpu.make_async_remote_copy(
        src_ref=first_out,
        dst_ref=shifted,
        send_sem=sh_sem.at[0],
        recv_sem=sh_sem.at[1],
        device_id=following,
        device_id_type=MESH,
    )
    relay.start()
    relay.wait_recv()
    stream[...] = jnp.where(depth == 0, fresh[half].astype(F32), shifted[...].astype(F32)).astype(BF16)
    layer(1, memory_out, totals_out)
    second_out[...] = total[...].astype(BF16)

    relay.wait_send()
    for phase in range(4):
        block_copy(phase, base + me, ag_send.at[phase, me], partner).wait_send()
        for chunk in range(CHUNKS):
            exchange_copy(phase, chunk).wait_send()

        def drain(step, _):
            target = peer(step)
            block_copy(phase, base + me, ag_send.at[phase, target], partner).wait_send()
            block_copy(phase, base + target, fw_send.at[phase, target], partner).wait_send()
            for chunk in range(CHUNKS):
                sum_copy(phase, chunk, target, me).wait_send()
            return 0

        lax.fori_loop(1, group, drain, 0)


def solution(mesh):
    n_layer, group = mesh.shape["layer"], mesh.shape["tp"]

    def body(acts, fresh, g_one, g_two, p_qkv, p_out, p_gu, p_down, memory, totals, logits):
        rows, width = acts.shape
        head = memory.shape[-1]
        ff = p_down.shape[0]
        blocks = 2 * group
        gate_up = jnp.concatenate([p_gu[:, 0], p_gu[:, 1]], axis=1)
        vmem = pl.BlockSpec(memory_space=pltpu.VMEM)
        hbm = pl.BlockSpec(memory_space=pl.ANY)
        dma = pltpu.SemaphoreType.DMA
        outs = pl.pallas_call(
            functools.partial(kernel, n_layer, group),
            out_shape=(
                jax.ShapeDtypeStruct((rows, width), BF16),
                jax.ShapeDtypeStruct((rows, width), BF16),
                jax.ShapeDtypeStruct((head, head), F32),
                jax.ShapeDtypeStruct((1, head), F32),
            ),
            in_specs=[vmem] * 4 + [hbm] * 4 + [vmem] * 3,
            out_specs=(vmem,) * 4,
            scratch_shapes=[
                pltpu.VMEM((width, 3 * head), BF16),
                pltpu.VMEM((head, width), BF16),
                pltpu.VMEM((width, 2 * ff), BF16),
                pltpu.VMEM((ff, width), BF16),
                pltpu.VMEM((4, blocks, rows, width), BF16),
                pltpu.VMEM((blocks, rows, 3 * head), BF16),
                pltpu.VMEM((blocks, rows, head), BF16),
                pltpu.VMEM((blocks, rows, ff), BF16),
                pltpu.VMEM((4, group, rows, width), BF16),
                pltpu.VMEM((4, group, rows, width), BF16),
                pltpu.VMEM((4, group, rows, width), BF16),
                pltpu.VMEM((4, group, rows, width), BF16),
                pltpu.VMEM((rows, width), BF16),
                pltpu.VMEM((rows, width), F32),
                pltpu.VMEM((rows, width), BF16),
                dma((4,)),
                dma((4, group)),
                dma((4, group)),
                dma((4, blocks)),
                dma((4, CHUNKS)),
                dma((4, CHUNKS)),
                dma((4, CHUNKS, group)),
                dma((4, CHUNKS, group)),
                dma((2,)),
            ],
            compiler_params=pltpu.CompilerParams(
                collective_id=0, has_side_effects=True, vmem_limit_bytes=44 * 1024 * 1024
            ),
        )(
            acts,
            fresh,
            g_one,
            g_two,
            p_qkv[0],
            p_out,
            gate_up,
            p_down,
            memory[0],
            totals,
            logits[:, None],
        )
        return outs[0], outs[1], outs[2][None], outs[3]

    both = ("layer", "tp")
    in_specs = (
        P(both, None),
        P(None, "tp", None),
        P(),
        P(),
        P(both, None, None),
        P(both, None),
        P(None, None, both),
        P(both, None),
        P(both, None, None),
        P(both, None),
        P(both),
    )
    out_specs = (P(both, None), P(both, None), P(both, None, None), P(both, None))
    return jax.shard_map(body, mesh=mesh, in_specs=in_specs, out_specs=out_specs, check_vma=False)
```

```python
import functools

import jax
import jax.numpy as jnp
from jax import lax
from jax.experimental import pallas as pl
from jax.experimental.pallas import tpu as pltpu
from jax.sharding import PartitionSpec as P

MESH = pl.DeviceIdType.MESH
F32 = jnp.float32
BF16 = jnp.bfloat16
CHUNKS = 2


def flat(value):
    blocks, rows, columns = value.shape
    if rows % 16 == 0 or value.dtype == F32:
        return value.reshape(blocks * rows, columns)
    return value.astype(F32).reshape(blocks * rows, columns).astype(value.dtype)


def norm(values, gain):
    scaled = values * lax.rsqrt(jnp.mean(values * values, axis=-1, keepdims=True) + 1e-05)
    return (scaled * gain).astype(BF16)


def lifted(values):
    return jnp.maximum(values, 0.0) + jnp.exp(jnp.minimum(values, 0.0))


def kernel(
    n_layer,
    group,
    acts_hbm,
    fresh_hbm,
    gain_first_hbm,
    gain_second_hbm,
    w_qkv_hbm,
    w_out_hbm,
    w_gu_hbm,
    w_down_hbm,
    memory_hbm,
    totals,
    logit,
    first_out,
    second_out,
    memory_out,
    totals_out,
    acts,
    fresh,
    gain_first,
    gain_second,
    w_qkv,
    w_out,
    w_gu,
    w_down,
    memory,
    gathered,
    qkv,
    blended,
    hidden,
    given,
    taken,
    summed,
    arrived,
    relayed,
    stream,
    total,
    shifted,
    w_sem,
    ag_send,
    fw_send,
    ag_recv,
    x_send,
    x_recv,
    r_send,
    r_recv,
    l_recv,
    sh_sem,
):
    place = lax.axis_index("layer")
    me = lax.axis_index("tp")
    half = lax.rem(place, 2)
    depth = lax.div(place, 2)
    base = half * group
    other_base = (1 - half) * group
    partner = (place + 1 - 2 * half, me)
    rows, width = acts.shape
    cols = width // CHUNKS
    head = memory.shape[-1]
    ff = w_down.shape[0]
    following = (lax.rem(place + 2, n_layer), me)
    previous = (lax.rem(place + n_layer - 2, n_layer), me)

    loads = [
        pltpu.make_async_copy(hbm, vmem, w_sem.at[k])
        for k, (hbm, vmem) in enumerate(
            [
                (acts_hbm, acts),
                (gain_first_hbm, gain_first),
                (w_qkv_hbm, w_qkv),
                (memory_hbm, memory),
                (w_out_hbm, w_out),
                (gain_second_hbm, gain_second),
                (w_gu_hbm, w_gu),
                (w_down_hbm, w_down),
                (fresh_hbm.at[half], fresh),
            ]
        )
    ]
    for copy in loads:
        copy.start()
    near = me + 1 - 2 * lax.rem(me, 2)
    mirror = group - 1 - me
    opposite = lax.rem(me + 2, group)
    inner = lax.rem(lax.div(me + 1, 2), 2)

    def peer(step):
        return lax.rem(me + step, group)

    barrier = pltpu.get_barrier_semaphore()
    for device in (partner, following, previous):
        pl.semaphore_signal(barrier, inc=1, device_id=device, device_id_type=MESH)

    def greet(step, _):
        pl.semaphore_signal(barrier, inc=1, device_id=(place, peer(step)), device_id_type=MESH)
        return 0

    lax.fori_loop(1, group, greet, 0)
    pl.semaphore_wait(barrier, 3 + group - 1)

    def block_copy(phase, slot, send_sem, device):
        return pltpu.make_async_remote_copy(
            src_ref=gathered.at[phase, slot],
            dst_ref=gathered.at[phase, slot],
            send_sem=send_sem,
            recv_sem=ag_recv.at[phase, slot],
            device_id=device,
            device_id_type=MESH,
        )

    def gather(phase, values, work):
        mine = base + me
        gathered[phase, mine] = values

        def send(step, _):
            target = peer(step)
            block_copy(phase, mine, ag_send.at[phase, target], (place, target)).start()
            return 0

        def send_to(target):
            block_copy(phase, mine, ag_send.at[phase, target], (place, target)).start()

        if group == 4:
            send_to(near + inner * (mirror - near))
            send_to(mirror + inner * (near - mirror))

            @pl.when(inner == 0)
            def _():
                send_to(opposite)
        else:
            lax.fori_loop(1, group, send, 0)
        block_copy(phase, mine, ag_send.at[phase, me], partner).start()
        if phase == 0:
            loads[2].wait()
        if phase == 1:
            loads[6].wait()
        work(mine)
        block_copy(phase, other_base + me, ag_send.at[phase, me], partner).wait_recv()
        work(other_base + me)

        order = [near + inner * (mirror - near), mirror + inner * (near - mirror), opposite]

        def forward(step, _):
            source = order[step - 1] if group == 4 else peer(group - step)
            slot = base + source
            block_copy(phase, slot, ag_send.at[phase, me], partner).wait_recv()
            if group == 4 and step == 1:

                @pl.when(inner == 1)
                def _():
                    block_copy(phase, slot, ag_send.at[phase, opposite], (place, near)).start()

            block_copy(phase, slot, fw_send.at[phase, source], partner).start()
            work(slot)
            return 0

        if group == 4:
            for step in range(1, 4):
                forward(step, 0)
        else:
            lax.fori_loop(1, group, forward, 0)

        def finish(step, _):
            source = order[step - 1] if group == 4 else peer(group - step)
            slot = other_base + source
            block_copy(phase, slot, ag_send.at[phase, me], partner).wait_recv()
            work(slot)
            return 0

        if group == 4:
            for step in range(1, 4):
                finish(step, 0)
        else:
            lax.fori_loop(1, group, finish, 0)

    def exchange_copy(phase, chunk):
        part = pl.ds(chunk * cols, cols)
        return pltpu.make_async_remote_copy(
            src_ref=given.at[phase, :, :, part],
            dst_ref=taken.at[phase, :, :, part],
            send_sem=x_send.at[phase, chunk],
            recv_sem=x_recv.at[phase, chunk],
            device_id=partner,
            device_id_type=MESH,
        )

    def sum_copy(phase, chunk, target, source):
        part = pl.ds(chunk * cols, cols)
        return pltpu.make_async_remote_copy(
            src_ref=summed.at[phase, target, :, part],
            dst_ref=arrived.at[phase, source, :, part],
            send_sem=r_send.at[phase, chunk, target],
            recv_sem=r_recv.at[phase, chunk, source],
            device_id=(place, target),
            device_id_type=MESH,
        )

    def relay_copy(phase, chunk):
        part = pl.ds(chunk * cols, cols)
        return pltpu.make_async_remote_copy(
            src_ref=summed.at[phase, opposite, :, part],
            dst_ref=relayed.at[phase, :, part],
            send_sem=r_send.at[phase, chunk, opposite],
            recv_sem=l_recv.at[phase, chunk],
            device_id=(place, near),
            device_id_type=MESH,
        )

    def reduce(phase, local, weight, between):
        theirs = flat(local[pl.ds(other_base, group)])
        ours = flat(local[pl.ds(base, group)])
        for chunk in range(CHUNKS):
            part = slice(chunk * cols, (chunk + 1) * cols)
            term = jnp.dot(theirs, weight[:, part], preferred_element_type=F32)
            given[phase, :, :, part] = term.reshape(group, rows, cols).astype(BF16)
            exchange_copy(phase, chunk).start()
        for chunk in range(CHUNKS):
            part = slice(chunk * cols, (chunk + 1) * cols)
            term = jnp.dot(ours, weight[:, part], preferred_element_type=F32)
            exchange_copy(phase, chunk).wait_recv()
            term = term.reshape(group, rows, cols) + taken[phase, :, :, part].astype(F32)
            summed[phase, :, :, part] = term.astype(BF16)

            def send(step, _):
                sum_copy(phase, chunk, peer(step), me).start()
                return 0

            if group == 4:

                @pl.when(inner == 0)
                def _():
                    relay_copy(phase, chunk).start()
                    sum_copy(phase, chunk, mirror, me).start()

                @pl.when(inner == 1)
                def _():
                    sum_copy(phase, chunk, opposite, me).start()

                sum_copy(phase, chunk, near, me).start()
            else:
                lax.fori_loop(1, group, send, 0)
        if group == 4:

            @pl.when(inner == 1)
            def _():
                for chunk in range(CHUNKS):
                    part = slice(chunk * cols, (chunk + 1) * cols)
                    relay_copy(phase, chunk).wait_recv()
                    term = summed[phase, mirror, :, part].astype(F32)
                    term += relayed[phase, :, part].astype(F32)
                    summed[phase, mirror, :, part] = term.astype(BF16)
                    sum_copy(phase, chunk, mirror, me).start()

        between()
        for chunk in range(CHUNKS):
            part = slice(chunk * cols, (chunk + 1) * cols)
            total[:, part] += summed[phase, me, :, part].astype(F32)

            def add(step, _):
                source = peer(group - step)
                sum_copy(phase, chunk, me, source).wait_recv()
                total[:, part] += arrived[phase, source, :, part].astype(F32)
                return 0

            def add_from(source):
                sum_copy(phase, chunk, me, source).wait_recv()
                total[:, part] += arrived[phase, source, :, part].astype(F32)

            if group == 4:
                add_from(near)
                add_from(mirror)

                @pl.when(inner == 0)
                def _():
                    add_from(opposite)
            else:
                lax.fori_loop(1, group, add, 0)

    def project(phase):
        def work(slot):
            qkv[slot] = lax.dot_general(
                gathered[phase, slot],
                w_qkv[...],
                (((1,), (1,)), ((), ())),
                preferred_element_type=F32,
            ).astype(BF16)

        return work

    def expand(phase):
        def work(slot):
            row_block = gathered[phase, slot]
            gate = jnp.dot(row_block, w_gu[:, 0].reshape(width, ff), preferred_element_type=F32)
            up = jnp.dot(row_block, w_gu[:, 1].reshape(width, ff), preferred_element_type=F32)
            hidden[slot] = (gate / (1.0 + jnp.exp(-gate)) * up).astype(BF16)

        return work

    def attend(memory_ref, totals_ref):
        all_rows = flat(qkv[...])
        seg = all_rows.shape[0]
        queries = all_rows[:, :head]
        keys = all_rows[:, head : 2 * head]
        values = all_rows[:, 2 * head :]
        scores = lax.dot_general(
            queries, keys, (((1,), (1,)), ((), ())), preferred_element_type=F32
        ) * head ** (-0.5)
        at_row = lax.broadcasted_iota(jnp.int32, (seg, seg), 0)
        at_col = lax.broadcasted_iota(jnp.int32, (seg, seg), 1)
        scores = jnp.where(at_row >= at_col, scores, -jnp.inf)
        powers = jnp.exp(scores - jnp.max(scores, axis=-1, keepdims=True))
        probs = (powers / jnp.sum(powers, axis=-1, keepdims=True)).astype(BF16)
        direct = jnp.dot(probs, values, preferred_element_type=F32)
        lifted_q = lifted(queries.astype(F32))
        numer = jnp.dot(
            lifted_q, memory_ref[...], preferred_element_type=F32, precision=lax.Precision.HIGHEST
        )
        denom = jnp.sum(lifted_q * totals_ref[...], axis=-1, keepdims=True)
        opened = 1.0 / (1.0 + jnp.exp(-logit[...]))
        mixed = opened * (numer / denom) + (1.0 - opened) * direct
        blended[...] = mixed.reshape(blended.shape).astype(BF16)

    def remember(memory_ref, totals_ref):
        all_rows = flat(qkv[...])
        lifted_k = lifted(all_rows[:, head : 2 * head].astype(F32))
        values = all_rows[:, 2 * head :].astype(F32)
        memory_out[...] = memory_ref[...] + lax.dot_general(
            lifted_k,
            values,
            (((0,), (0,)), ((), ())),
            preferred_element_type=F32,
            precision=lax.Precision.HIGHEST,
        )
        totals_out[...] = totals_ref[...] + jnp.sum(lifted_k, axis=0, keepdims=True)

    def layer(turn, memory_ref, totals_ref):
        first, second = 2 * turn, 2 * turn + 1
        start = stream[...].astype(F32)
        gather(first, norm(start, gain_first[pl.ds(depth, 1), :]), project(first))
        total[...] = start
        if turn == 0:
            loads[3].wait()
        attend(memory_ref, totals_ref)
        if turn == 0:
            loads[4].wait()
            loads[5].wait()
        reduce(first, blended, w_out, lambda: remember(memory_ref, totals_ref))
        middle = total[...].astype(BF16).astype(F32)
        gather_two = norm(middle, gain_second[pl.ds(depth, 1), :])
        total[...] = middle
        if turn == 0:
            gather(second, gather_two, expand(second))
            loads[7].wait()
        else:
            gather(second, gather_two, expand(second))
        reduce(second, hidden, w_down, lambda: None)

    loads[0].wait()
    loads[1].wait()
    stream[...] = acts[...]
    layer(0, memory, totals)
    first_out[...] = total[...].astype(BF16)
    relay = pltpu.make_async_remote_copy(
        src_ref=first_out,
        dst_ref=shifted,
        send_sem=sh_sem.at[0],
        recv_sem=sh_sem.at[1],
        device_id=following,
        device_id_type=MESH,
    )
    relay.start()
    loads[8].wait()
    relay.wait_recv()
    stream[...] = jnp.where(depth == 0, fresh[...].astype(F32), shifted[...].astype(F32)).astype(BF16)
    layer(1, memory_out, totals_out)
    second_out[...] = total[...].astype(BF16)

    relay.wait_send()
    for phase in range(4):
        block_copy(phase, base + me, ag_send.at[phase, me], partner).wait_send()
        for chunk in range(CHUNKS):
            exchange_copy(phase, chunk).wait_send()

        def drain(step, _):
            target = peer(step)
            block_copy(phase, base + me, ag_send.at[phase, target], partner).wait_send()
            block_copy(phase, base + target, fw_send.at[phase, target], partner).wait_send()
            for chunk in range(CHUNKS):
                sum_copy(phase, chunk, target, me).wait_send()
            return 0

        lax.fori_loop(1, group, drain, 0)


def deliver(*refs):
    sources, targets, sems = refs[:4], refs[4:8], refs[8]
    copies = [
        pltpu.make_async_copy(source, target, sems.at[k])
        for k, (source, target) in enumerate(zip(sources, targets))
    ]
    for copy in copies:
        copy.start()
    for copy in copies:
        copy.wait()


def relaid(weight):
    width, two, ff = weight.shape
    block = 256
    same = lax.broadcasted_iota(jnp.int32, (block, block), 0) == lax.broadcasted_iota(
        jnp.int32, (block, block), 1
    )
    cut = weight.reshape(width // block, block, two, ff)
    return jnp.einsum("bdtf,de->btef", cut, same.astype(BF16), preferred_element_type=BF16)


def solution(mesh):
    n_layer, group = mesh.shape["layer"], mesh.shape["tp"]

    def body(acts, fresh, g_one, g_two, p_qkv, p_out, p_gu, p_down, memory, totals, logits):
        rows, width = acts.shape
        head = memory.shape[-1]
        ff = p_down.shape[0]
        blocks = 2 * group
        gate_up = relaid(p_gu)
        vmem = pl.BlockSpec(memory_space=pltpu.VMEM)
        hbm = pl.BlockSpec(memory_space=pl.ANY)
        dma = pltpu.SemaphoreType.DMA
        outs = pl.pallas_call(
            functools.partial(kernel, n_layer, group),
            out_shape=(
                jax.ShapeDtypeStruct((rows, width), BF16),
                jax.ShapeDtypeStruct((rows, width), BF16),
                jax.ShapeDtypeStruct((head, head), F32),
                jax.ShapeDtypeStruct((1, head), F32),
            ),
            in_specs=[hbm] * 9 + [vmem] * 2,
            out_specs=(vmem,) * 4,
            scratch_shapes=[
                pltpu.VMEM((rows, width), BF16),
                pltpu.VMEM((rows, width), BF16),
                pltpu.VMEM(g_one.shape, F32),
                pltpu.VMEM(g_two.shape, F32),
                pltpu.VMEM((3 * head, width), BF16),
                pltpu.VMEM((head, width), BF16),
                pltpu.VMEM(gate_up.shape, BF16),
                pltpu.VMEM((ff, width), BF16),
                pltpu.VMEM((head, head), F32),
                pltpu.VMEM((4, blocks, rows, width), BF16),
                pltpu.VMEM((blocks, rows, 3 * head), BF16),
                pltpu.VMEM((blocks, rows, head), BF16),
                pltpu.VMEM((blocks, rows, ff), BF16),
                pltpu.VMEM((4, group, rows, width), BF16),
                pltpu.VMEM((4, group, rows, width), BF16),
                pltpu.VMEM((4, group, rows, width), BF16),
                pltpu.VMEM((4, group, rows, width), BF16),
                pltpu.VMEM((4, rows, width), BF16),
                pltpu.VMEM((rows, width), BF16),
                pltpu.VMEM((rows, width), F32),
                pltpu.VMEM((rows, width), BF16),
                dma((9,)),
                dma((4, group)),
                dma((4, group)),
                dma((4, blocks)),
                dma((4, CHUNKS)),
                dma((4, CHUNKS)),
                dma((4, CHUNKS, group)),
                dma((4, CHUNKS, group)),
                dma((4, CHUNKS)),
                dma((2,)),
            ],
            compiler_params=pltpu.CompilerParams(
                collective_id=0, has_side_effects=True, vmem_limit_bytes=58 * 1024 * 1024
            ),
        )(
            acts,
            fresh,
            g_one,
            g_two,
            jnp.swapaxes(p_qkv[0], 0, 1),
            p_out,
            gate_up,
            p_down,
            memory[0],
            totals,
            logits[:, None],
        )
        first, second, after, norms = pl.pallas_call(
            deliver,
            out_shape=[jax.ShapeDtypeStruct(o.shape, o.dtype) for o in outs],
            in_specs=[hbm] * 4,
            out_specs=[hbm] * 4,
            scratch_shapes=[dma((4,))],
        )(*outs)
        return first, second, after[None], norms

    both = ("layer", "tp")
    in_specs = (
        P(both, None),
        P(None, "tp", None),
        P(),
        P(),
        P(both, None, None),
        P(both, None),
        P(None, None, both),
        P(both, None),
        P(both, None, None),
        P(both, None),
        P(both),
    )
    out_specs = (P(both, None), P(both, None), P(both, None, None), P(both, None))
    return jax.shard_map(body, mesh=mesh, in_specs=in_specs, out_specs=out_specs, check_vma=False)
```

```python
import functools

import jax
import jax.numpy as jnp
from jax import lax
from jax.experimental import pallas as pl
from jax.experimental.pallas import tpu as pltpu
from jax.sharding import PartitionSpec as P

MESH = pl.DeviceIdType.MESH
F32 = jnp.float32
BF16 = jnp.bfloat16
CHUNKS = 2


def flat(value):
    blocks, rows, columns = value.shape
    if rows % 16 == 0 or value.dtype == F32:
        return value.reshape(blocks * rows, columns)
    return value.astype(F32).reshape(blocks * rows, columns).astype(value.dtype)


def norm(values, gain):
    scaled = values * lax.rsqrt(jnp.mean(values * values, axis=-1, keepdims=True) + 1e-05)
    return (scaled * gain).astype(BF16)


def lifted(values):
    return jnp.maximum(values, 0.0) + jnp.exp(jnp.minimum(values, 0.0))


def kernel(
    n_layer,
    group,
    acts_hbm,
    fresh_hbm,
    gain_first_hbm,
    gain_second_hbm,
    w_qkv_hbm,
    w_out_hbm,
    w_gu_hbm,
    w_down_hbm,
    memory_hbm,
    totals,
    logit,
    first_out,
    second_out,
    memory_out,
    totals_out,
    acts,
    fresh,
    gain_first,
    gain_second,
    w_qkv,
    w_out,
    w_gu,
    w_down,
    memory,
    gathered,
    qkv,
    blended,
    hidden,
    given,
    taken,
    summed,
    arrived,
    relayed,
    stream,
    total,
    shifted,
    w_sem,
    ag_send,
    fw_send,
    ag_recv,
    x_send,
    x_recv,
    r_send,
    r_recv,
    l_recv,
    e_send,
    e_recv,
    sh_sem,
):
    place = lax.axis_index("layer")
    me = lax.axis_index("tp")
    half = lax.rem(place, 2)
    depth = lax.div(place, 2)
    base = half * group
    other_base = (1 - half) * group
    partner = (place + 1 - 2 * half, me)
    rows, width = acts.shape
    cols = width // CHUNKS
    head = memory.shape[-1]
    ff = w_down.shape[0]
    following = (lax.rem(place + 2, n_layer), me)
    previous = (lax.rem(place + n_layer - 2, n_layer), me)

    loads = [
        pltpu.make_async_copy(hbm, vmem, w_sem.at[k])
        for k, (hbm, vmem) in enumerate(
            [
                (acts_hbm, acts),
                (gain_first_hbm, gain_first),
                (w_qkv_hbm, w_qkv),
                (memory_hbm, memory),
                (w_out_hbm, w_out),
                (gain_second_hbm, gain_second),
                (w_gu_hbm, w_gu),
                (w_down_hbm, w_down),
                (fresh_hbm.at[half], fresh),
            ]
        )
    ]
    for copy in loads:
        copy.start()
    near = me + 1 - 2 * lax.rem(me, 2)
    mirror = group - 1 - me
    opposite = lax.rem(me + 2, group)
    inner = lax.rem(lax.div(me + 1, 2), 2)

    def peer(step):
        return lax.rem(me + step, group)

    barrier = pltpu.get_barrier_semaphore()
    for device in (partner, following, previous):
        pl.semaphore_signal(barrier, inc=1, device_id=device, device_id_type=MESH)

    def greet(step, _):
        pl.semaphore_signal(barrier, inc=1, device_id=(place, peer(step)), device_id_type=MESH)
        return 0

    lax.fori_loop(1, group, greet, 0)
    pl.semaphore_wait(barrier, 3 + group - 1)

    def block_copy(phase, slot, send_sem, device):
        return pltpu.make_async_remote_copy(
            src_ref=gathered.at[phase, slot],
            dst_ref=gathered.at[phase, slot],
            send_sem=send_sem,
            recv_sem=ag_recv.at[phase, slot],
            device_id=device,
            device_id_type=MESH,
        )

    order = [near + inner * (mirror - near), mirror + inner * (near - mirror), opposite]

    def announce(phase, values):
        mine = base + me
        gathered[phase, mine] = values

        def send(step, _):
            target = peer(step)
            block_copy(phase, mine, ag_send.at[phase, target], (place, target)).start()
            return 0

        def send_to(target):
            block_copy(phase, mine, ag_send.at[phase, target], (place, target)).start()

        if group == 4:
            send_to(near + inner * (mirror - near))
            send_to(mirror + inner * (near - mirror))

            @pl.when(inner == 0)
            def _():
                send_to(opposite)
        else:
            lax.fori_loop(1, group, send, 0)
        block_copy(phase, mine, ag_send.at[phase, me], partner).start()
        if phase == 0:
            loads[2].wait()
        if phase == 1:
            loads[6].wait()

    def pass_on(phase, source, step):
        slot = base + source
        block_copy(phase, slot, ag_send.at[phase, me], partner).wait_recv()
        if group == 4 and step == 1:

            @pl.when(inner == 1)
            def _():
                block_copy(phase, slot, ag_send.at[phase, opposite], (place, near)).start()

        block_copy(phase, slot, fw_send.at[phase, source], partner).start()

    def gather(phase, values, work):
        announce(phase, values)
        work(base + me)
        block_copy(phase, other_base + me, ag_send.at[phase, me], partner).wait_recv()
        work(other_base + me)

        def forward(step, _):
            source = order[step - 1] if group == 4 else peer(group - step)
            pass_on(phase, source, step)
            work(base + source)
            return 0

        if group == 4:
            for step in range(1, 4):
                forward(step, 0)
        else:
            lax.fori_loop(1, group, forward, 0)

        def finish(step, _):
            source = order[step - 1] if group == 4 else peer(group - step)
            slot = other_base + source
            block_copy(phase, slot, ag_send.at[phase, me], partner).wait_recv()
            work(slot)
            return 0

        if group == 4:
            for step in range(1, 4):
                finish(step, 0)
        else:
            lax.fori_loop(1, group, finish, 0)

    def exchange_copy(phase, chunk):
        part = pl.ds(chunk * cols, cols)
        return pltpu.make_async_remote_copy(
            src_ref=given.at[phase, :, :, part],
            dst_ref=taken.at[phase, :, :, part],
            send_sem=x_send.at[phase, chunk],
            recv_sem=x_recv.at[phase, chunk],
            device_id=partner,
            device_id_type=MESH,
        )

    def sum_copy(phase, chunk, target, source):
        part = pl.ds(chunk * cols, cols)
        return pltpu.make_async_remote_copy(
            src_ref=summed.at[phase, target, :, part],
            dst_ref=arrived.at[phase, source, :, part],
            send_sem=r_send.at[phase, chunk, target],
            recv_sem=r_recv.at[phase, chunk, source],
            device_id=(place, target),
            device_id_type=MESH,
        )

    def relay_copy(phase, chunk):
        part = pl.ds(chunk * cols, cols)
        return pltpu.make_async_remote_copy(
            src_ref=summed.at[phase, opposite, :, part],
            dst_ref=relayed.at[phase, :, part],
            send_sem=r_send.at[phase, chunk, opposite],
            recv_sem=l_recv.at[phase, chunk],
            device_id=(place, near),
            device_id_type=MESH,
        )

    def reduce(phase, local, weight, between):
        theirs = flat(local[pl.ds(other_base, group)])
        ours = flat(local[pl.ds(base, group)])
        for chunk in range(CHUNKS):
            part = slice(chunk * cols, (chunk + 1) * cols)
            term = jnp.dot(theirs, weight[:, part], preferred_element_type=F32)
            given[phase, :, :, part] = term.reshape(group, rows, cols).astype(BF16)
            exchange_copy(phase, chunk).start()
        for chunk in range(CHUNKS):
            part = slice(chunk * cols, (chunk + 1) * cols)
            term = jnp.dot(ours, weight[:, part], preferred_element_type=F32)
            exchange_copy(phase, chunk).wait_recv()
            term = term.reshape(group, rows, cols) + taken[phase, :, :, part].astype(F32)
            summed[phase, :, :, part] = term.astype(BF16)

            def send(step, _):
                sum_copy(phase, chunk, peer(step), me).start()
                return 0

            if group == 4:

                @pl.when(inner == 0)
                def _():
                    relay_copy(phase, chunk).start()
                    sum_copy(phase, chunk, mirror, me).start()

                @pl.when(inner == 1)
                def _():
                    sum_copy(phase, chunk, opposite, me).start()

                sum_copy(phase, chunk, near, me).start()
            else:
                lax.fori_loop(1, group, send, 0)
        if group == 4:

            @pl.when(inner == 1)
            def _():
                for chunk in range(CHUNKS):
                    part = slice(chunk * cols, (chunk + 1) * cols)
                    relay_copy(phase, chunk).wait_recv()
                    term = summed[phase, mirror, :, part].astype(F32)
                    term += relayed[phase, :, part].astype(F32)
                    summed[phase, mirror, :, part] = term.astype(BF16)
                    sum_copy(phase, chunk, mirror, me).start()

        between()
        for chunk in range(CHUNKS):
            part = slice(chunk * cols, (chunk + 1) * cols)
            total[:, part] += summed[phase, me, :, part].astype(F32)

            def add(step, _):
                source = peer(group - step)
                sum_copy(phase, chunk, me, source).wait_recv()
                total[:, part] += arrived[phase, source, :, part].astype(F32)
                return 0

            def add_from(source):
                sum_copy(phase, chunk, me, source).wait_recv()
                total[:, part] += arrived[phase, source, :, part].astype(F32)

            if group == 4:
                add_from(near)
                add_from(mirror)

                @pl.when(inner == 0)
                def _():
                    add_from(opposite)
            else:
                lax.fori_loop(1, group, add, 0)

    def project(phase):
        def work(slot):
            qkv[slot] = lax.dot_general(
                gathered[phase, slot],
                w_qkv[...],
                (((1,), (1,)), ((), ())),
                preferred_element_type=F32,
            ).astype(BF16)

        return work

    def expand(phase):
        def work(slot):
            row_block = gathered[phase, slot]
            gate = jnp.dot(row_block, w_gu[:, 0].reshape(width, ff), preferred_element_type=F32)
            up = jnp.dot(row_block, w_gu[:, 1].reshape(width, ff), preferred_element_type=F32)
            hidden[slot] = (gate / (1.0 + jnp.exp(-gate)) * up).astype(BF16)

        return work

    def swap_copy(phase, source):
        return pltpu.make_async_remote_copy(
            src_ref=given.at[phase, source],
            dst_ref=taken.at[phase, source],
            send_sem=e_send.at[phase, source],
            recv_sem=e_recv.at[phase, source],
            device_id=partner,
            device_id_type=MESH,
        )

    def whole_copy(phase, target, source):
        return pltpu.make_async_remote_copy(
            src_ref=summed.at[phase, target],
            dst_ref=arrived.at[phase, source],
            send_sem=r_send.at[phase, 0, target],
            recv_sem=r_recv.at[phase, 0, source],
            device_id=(place, target),
            device_id_type=MESH,
        )

    def feed(phase, values):
        work = expand(phase)
        announce(phase, values)
        work(base + me)
        if phase == 1:
            loads[7].wait()

        def give(source):
            slot = other_base + source
            block_copy(phase, slot, ag_send.at[phase, me], partner).wait_recv()
            work(slot)
            term = jnp.dot(hidden[slot], w_down[...], preferred_element_type=F32)
            given[phase, source] = term.astype(BF16)
            swap_copy(phase, source).start()

        def take(source):
            term = jnp.dot(hidden[base + source], w_down[...], preferred_element_type=F32)
            swap_copy(phase, source).wait_recv()
            return term + taken[phase, source].astype(F32)

        def give_back(source):
            summed[phase, source] = take(source).astype(BF16)
            whole_copy(phase, source, me).start()

        give(me)
        for step in range(1, 4):
            pass_on(phase, order[step - 1], step)
            work(base + order[step - 1])
            if step > 1:
                give_back(order[step - 2])
            give(order[step - 1])
        give_back(order[2])
        total[...] += take(me)
        for source in order:
            whole_copy(phase, me, source).wait_recv()
            total[...] += arrived[phase, source].astype(F32)

    def attend(memory_ref, totals_ref):
        all_rows = flat(qkv[...])
        seg = all_rows.shape[0]
        queries = all_rows[:, :head]
        keys = all_rows[:, head : 2 * head]
        values = all_rows[:, 2 * head :]
        scores = lax.dot_general(
            queries, keys, (((1,), (1,)), ((), ())), preferred_element_type=F32
        ) * head ** (-0.5)
        at_row = lax.broadcasted_iota(jnp.int32, (seg, seg), 0)
        at_col = lax.broadcasted_iota(jnp.int32, (seg, seg), 1)
        scores = jnp.where(at_row >= at_col, scores, -jnp.inf)
        powers = jnp.exp(scores - jnp.max(scores, axis=-1, keepdims=True))
        probs = (powers / jnp.sum(powers, axis=-1, keepdims=True)).astype(BF16)
        direct = jnp.dot(probs, values, preferred_element_type=F32)
        lifted_q = lifted(queries.astype(F32))
        numer = jnp.dot(
            lifted_q, memory_ref[...], preferred_element_type=F32, precision=lax.Precision.HIGHEST
        )
        denom = jnp.sum(lifted_q * totals_ref[...], axis=-1, keepdims=True)
        opened = 1.0 / (1.0 + jnp.exp(-logit[...]))
        mixed = opened * (numer / denom) + (1.0 - opened) * direct
        blended[...] = mixed.reshape(blended.shape).astype(BF16)

    def remember(memory_ref, totals_ref):
        all_rows = flat(qkv[...])
        lifted_k = lifted(all_rows[:, head : 2 * head].astype(F32))
        values = all_rows[:, 2 * head :].astype(F32)
        memory_out[...] = memory_ref[...] + lax.dot_general(
            lifted_k,
            values,
            (((0,), (0,)), ((), ())),
            preferred_element_type=F32,
            precision=lax.Precision.HIGHEST,
        )
        totals_out[...] = totals_ref[...] + jnp.sum(lifted_k, axis=0, keepdims=True)

    def layer(turn, memory_ref, totals_ref):
        first, second = 2 * turn, 2 * turn + 1
        start = stream[...].astype(F32)
        gather(first, norm(start, gain_first[pl.ds(depth, 1), :]), project(first))
        total[...] = start
        if turn == 0:
            loads[3].wait()
        attend(memory_ref, totals_ref)
        if turn == 0:
            loads[4].wait()
            loads[5].wait()
        reduce(first, blended, w_out, lambda: remember(memory_ref, totals_ref))
        middle = total[...].astype(BF16).astype(F32)
        gather_two = norm(middle, gain_second[pl.ds(depth, 1), :])
        total[...] = middle
        if group == 4:
            feed(second, gather_two)
        else:
            gather(second, gather_two, expand(second))
            if turn == 0:
                loads[7].wait()
            reduce(second, hidden, w_down, lambda: None)

    loads[0].wait()
    loads[1].wait()
    stream[...] = acts[...]
    layer(0, memory, totals)
    first_out[...] = total[...].astype(BF16)
    relay = pltpu.make_async_remote_copy(
        src_ref=first_out,
        dst_ref=shifted,
        send_sem=sh_sem.at[0],
        recv_sem=sh_sem.at[1],
        device_id=following,
        device_id_type=MESH,
    )
    relay.start()
    loads[8].wait()
    relay.wait_recv()
    stream[...] = jnp.where(depth == 0, fresh[...].astype(F32), shifted[...].astype(F32)).astype(BF16)
    layer(1, memory_out, totals_out)
    second_out[...] = total[...].astype(BF16)

    relay.wait_send()
    for phase in range(4):
        block_copy(phase, base + me, ag_send.at[phase, me], partner).wait_send()
        piped = group == 4 and phase % 2 == 1
        if piped:
            swap_copy(phase, me).wait_send()
        else:
            for chunk in range(CHUNKS):
                exchange_copy(phase, chunk).wait_send()

        def drain(step, _):
            target = peer(step)
            block_copy(phase, base + me, ag_send.at[phase, target], partner).wait_send()
            block_copy(phase, base + target, fw_send.at[phase, target], partner).wait_send()
            if piped:
                swap_copy(phase, target).wait_send()
                whole_copy(phase, target, me).wait_send()
            else:
                for chunk in range(CHUNKS):
                    sum_copy(phase, chunk, target, me).wait_send()
            return 0

        lax.fori_loop(1, group, drain, 0)


def deliver(*refs):
    sources, targets, sems = refs[:4], refs[4:8], refs[8]
    copies = [
        pltpu.make_async_copy(source, target, sems.at[k])
        for k, (source, target) in enumerate(zip(sources, targets))
    ]
    for copy in copies:
        copy.start()
    for copy in copies:
        copy.wait()


def relaid(weight):
    width, two, ff = weight.shape
    block = 256
    same = lax.broadcasted_iota(jnp.int32, (block, block), 0) == lax.broadcasted_iota(
        jnp.int32, (block, block), 1
    )
    cut = weight.reshape(width // block, block, two, ff)
    return jnp.einsum("bdtf,de->btef", cut, same.astype(BF16), preferred_element_type=BF16)


def solution(mesh):
    n_layer, group = mesh.shape["layer"], mesh.shape["tp"]

    def body(acts, fresh, g_one, g_two, p_qkv, p_out, p_gu, p_down, memory, totals, logits):
        rows, width = acts.shape
        head = memory.shape[-1]
        ff = p_down.shape[0]
        blocks = 2 * group
        gate_up = relaid(p_gu)
        vmem = pl.BlockSpec(memory_space=pltpu.VMEM)
        hbm = pl.BlockSpec(memory_space=pl.ANY)
        dma = pltpu.SemaphoreType.DMA
        outs = pl.pallas_call(
            functools.partial(kernel, n_layer, group),
            out_shape=(
                jax.ShapeDtypeStruct((rows, width), BF16),
                jax.ShapeDtypeStruct((rows, width), BF16),
                jax.ShapeDtypeStruct((head, head), F32),
                jax.ShapeDtypeStruct((1, head), F32),
            ),
            in_specs=[hbm] * 9 + [vmem] * 2,
            out_specs=(vmem,) * 4,
            scratch_shapes=[
                pltpu.VMEM((rows, width), BF16),
                pltpu.VMEM((rows, width), BF16),
                pltpu.VMEM(g_one.shape, F32),
                pltpu.VMEM(g_two.shape, F32),
                pltpu.VMEM((3 * head, width), BF16),
                pltpu.VMEM((head, width), BF16),
                pltpu.VMEM(gate_up.shape, BF16),
                pltpu.VMEM((ff, width), BF16),
                pltpu.VMEM((head, head), F32),
                pltpu.VMEM((4, blocks, rows, width), BF16),
                pltpu.VMEM((blocks, rows, 3 * head), BF16),
                pltpu.VMEM((blocks, rows, head), BF16),
                pltpu.VMEM((blocks, rows, ff), BF16),
                pltpu.VMEM((4, group, rows, width), BF16),
                pltpu.VMEM((4, group, rows, width), BF16),
                pltpu.VMEM((4, group, rows, width), BF16),
                pltpu.VMEM((4, group, rows, width), BF16),
                pltpu.VMEM((4, rows, width), BF16),
                pltpu.VMEM((rows, width), BF16),
                pltpu.VMEM((rows, width), F32),
                pltpu.VMEM((rows, width), BF16),
                dma((9,)),
                dma((4, group)),
                dma((4, group)),
                dma((4, blocks)),
                dma((4, CHUNKS)),
                dma((4, CHUNKS)),
                dma((4, CHUNKS, group)),
                dma((4, CHUNKS, group)),
                dma((4, CHUNKS)),
                dma((4, group)),
                dma((4, group)),
                dma((2,)),
            ],
            compiler_params=pltpu.CompilerParams(
                collective_id=0, has_side_effects=True, vmem_limit_bytes=58 * 1024 * 1024
            ),
        )(
            acts,
            fresh,
            g_one,
            g_two,
            jnp.swapaxes(p_qkv[0], 0, 1),
            p_out,
            gate_up,
            p_down,
            memory[0],
            totals,
            logits[:, None],
        )
        first, second, after, norms = pl.pallas_call(
            deliver,
            out_shape=[jax.ShapeDtypeStruct(o.shape, o.dtype) for o in outs],
            in_specs=[vmem] * 4,
            out_specs=[hbm] * 4,
            scratch_shapes=[dma((4,))],
        )(*outs)
        return first, second, after[None], norms

    both = ("layer", "tp")
    in_specs = (
        P(both, None),
        P(None, "tp", None),
        P(),
        P(),
        P(both, None, None),
        P(both, None),
        P(None, None, both),
        P(both, None),
        P(both, None, None),
        P(both, None),
        P(both),
    )
    out_specs = (P(both, None), P(both, None), P(both, None, None), P(both, None))
    return jax.shard_map(body, mesh=mesh, in_specs=in_specs, out_specs=out_specs, check_vma=False)
```

```python
import functools

import jax
import jax.numpy as jnp
from jax import lax
from jax.experimental import pallas as pl
from jax.experimental.pallas import tpu as pltpu
from jax.sharding import PartitionSpec as P

MESH = pl.DeviceIdType.MESH
F32 = jnp.float32
BF16 = jnp.bfloat16
CHUNKS = 4


def flat(value):
    blocks, rows, columns = value.shape
    if rows % 16 == 0 or value.dtype == F32:
        return value.reshape(blocks * rows, columns)
    return value.astype(F32).reshape(blocks * rows, columns).astype(value.dtype)


def norm(values, gain):
    scaled = values * lax.rsqrt(jnp.mean(values * values, axis=-1, keepdims=True) + 1e-05)
    return (scaled * gain).astype(BF16)


def lifted(values):
    return jnp.maximum(values, 0.0) + jnp.exp(jnp.minimum(values, 0.0))


def kernel(
    n_layer,
    group,
    acts_hbm,
    fresh_hbm,
    gain_first_hbm,
    gain_second_hbm,
    w_qkv_hbm,
    w_out_hbm,
    w_gu_hbm,
    w_down_hbm,
    memory_hbm,
    totals,
    logit,
    first_out,
    second_out,
    memory_out,
    totals_out,
    acts,
    fresh,
    gain_first,
    gain_second,
    w_qkv,
    w_out,
    w_gu,
    w_down,
    memory,
    gathered,
    qkv,
    blended,
    hidden,
    given,
    taken,
    summed,
    arrived,
    relayed,
    stream,
    total,
    shifted,
    w_sem,
    ag_send,
    fw_send,
    ag_recv,
    x_send,
    x_recv,
    r_send,
    r_recv,
    l_recv,
    e_send,
    e_recv,
    sh_sem,
):
    place = lax.axis_index("layer")
    me = lax.axis_index("tp")
    half = lax.rem(place, 2)
    depth = lax.div(place, 2)
    base = half * group
    other_base = (1 - half) * group
    partner = (place + 1 - 2 * half, me)
    rows, width = acts.shape
    cols = width // CHUNKS
    head = memory.shape[-1]
    ff = w_down.shape[0]
    following = (lax.rem(place + 2, n_layer), me)
    previous = (lax.rem(place + n_layer - 2, n_layer), me)

    loads = [
        pltpu.make_async_copy(hbm, vmem, w_sem.at[k])
        for k, (hbm, vmem) in enumerate(
            [
                (acts_hbm, acts),
                (gain_first_hbm, gain_first),
                (w_qkv_hbm, w_qkv),
                (memory_hbm, memory),
                (w_out_hbm, w_out),
                (gain_second_hbm, gain_second),
                (w_gu_hbm, w_gu),
                (w_down_hbm, w_down),
                (fresh_hbm.at[half], fresh),
            ]
        )
    ]
    for copy in loads:
        copy.start()
    near = me + 1 - 2 * lax.rem(me, 2)
    mirror = group - 1 - me
    opposite = lax.rem(me + 2, group)
    inner = lax.rem(lax.div(me + 1, 2), 2)

    def peer(step):
        return lax.rem(me + step, group)

    barrier = pltpu.get_barrier_semaphore()
    for device in (partner, following, previous):
        pl.semaphore_signal(barrier, inc=1, device_id=device, device_id_type=MESH)

    def greet(step, _):
        pl.semaphore_signal(barrier, inc=1, device_id=(place, peer(step)), device_id_type=MESH)
        return 0

    lax.fori_loop(1, group, greet, 0)
    pl.semaphore_wait(barrier, 3 + group - 1)

    def block_copy(phase, slot, send_sem, device):
        return pltpu.make_async_remote_copy(
            src_ref=gathered.at[phase, slot],
            dst_ref=gathered.at[phase, slot],
            send_sem=send_sem,
            recv_sem=ag_recv.at[phase, slot],
            device_id=device,
            device_id_type=MESH,
        )

    order = [near + inner * (mirror - near), mirror + inner * (near - mirror), opposite]

    def announce(phase, values):
        mine = base + me
        gathered[phase, mine] = values

        def send(step, _):
            target = peer(step)
            block_copy(phase, mine, ag_send.at[phase, target], (place, target)).start()
            return 0

        def send_to(target):
            block_copy(phase, mine, ag_send.at[phase, target], (place, target)).start()

        if group == 4:
            send_to(near + inner * (mirror - near))
            send_to(mirror + inner * (near - mirror))

            @pl.when(inner == 0)
            def _():
                send_to(opposite)
        else:
            lax.fori_loop(1, group, send, 0)
        block_copy(phase, mine, ag_send.at[phase, me], partner).start()
        if phase == 0:
            loads[2].wait()
        if phase == 1:
            loads[6].wait()

    def pass_on(phase, source, step):
        slot = base + source
        block_copy(phase, slot, ag_send.at[phase, me], partner).wait_recv()
        if group == 4 and step == 1:

            @pl.when(inner == 1)
            def _():
                block_copy(phase, slot, ag_send.at[phase, opposite], (place, near)).start()

        block_copy(phase, slot, fw_send.at[phase, source], partner).start()

    def gather(phase, values, work):
        announce(phase, values)
        work(base + me)
        block_copy(phase, other_base + me, ag_send.at[phase, me], partner).wait_recv()
        work(other_base + me)

        def forward(step, _):
            source = order[step - 1] if group == 4 else peer(group - step)
            pass_on(phase, source, step)
            work(base + source)
            return 0

        if group == 4:
            for step in range(1, 4):
                forward(step, 0)
        else:
            lax.fori_loop(1, group, forward, 0)

        def finish(step, _):
            source = order[step - 1] if group == 4 else peer(group - step)
            slot = other_base + source
            block_copy(phase, slot, ag_send.at[phase, me], partner).wait_recv()
            work(slot)
            return 0

        if group == 4:
            for step in range(1, 4):
                finish(step, 0)
        else:
            lax.fori_loop(1, group, finish, 0)

    def exchange_copy(phase, chunk):
        part = pl.ds(chunk * cols, cols)
        return pltpu.make_async_remote_copy(
            src_ref=given.at[phase, :, :, part],
            dst_ref=taken.at[phase, :, :, part],
            send_sem=x_send.at[phase, chunk],
            recv_sem=x_recv.at[phase, chunk],
            device_id=partner,
            device_id_type=MESH,
        )

    def sum_copy(phase, chunk, target, source):
        part = pl.ds(chunk * cols, cols)
        return pltpu.make_async_remote_copy(
            src_ref=summed.at[phase, target, :, part],
            dst_ref=arrived.at[phase, source, :, part],
            send_sem=r_send.at[phase, chunk, target],
            recv_sem=r_recv.at[phase, chunk, source],
            device_id=(place, target),
            device_id_type=MESH,
        )

    def relay_copy(phase, chunk):
        part = pl.ds(chunk * cols, cols)
        return pltpu.make_async_remote_copy(
            src_ref=summed.at[phase, opposite, :, part],
            dst_ref=relayed.at[phase, :, part],
            send_sem=r_send.at[phase, chunk, opposite],
            recv_sem=l_recv.at[phase, chunk],
            device_id=(place, near),
            device_id_type=MESH,
        )

    def reduce(phase, local, weight, between):
        theirs = flat(local[pl.ds(other_base, group)])
        ours = flat(local[pl.ds(base, group)])
        for chunk in range(CHUNKS):
            part = slice(chunk * cols, (chunk + 1) * cols)
            term = jnp.dot(theirs, weight[:, part], preferred_element_type=F32)
            given[phase, :, :, part] = term.reshape(group, rows, cols).astype(BF16)
            exchange_copy(phase, chunk).start()
        for chunk in range(CHUNKS):
            part = slice(chunk * cols, (chunk + 1) * cols)
            term = jnp.dot(ours, weight[:, part], preferred_element_type=F32)
            exchange_copy(phase, chunk).wait_recv()
            term = term.reshape(group, rows, cols) + taken[phase, :, :, part].astype(F32)
            summed[phase, :, :, part] = term.astype(BF16)

            def send(step, _):
                sum_copy(phase, chunk, peer(step), me).start()
                return 0

            if group == 4:

                @pl.when(inner == 0)
                def _():
                    relay_copy(phase, chunk).start()
                    sum_copy(phase, chunk, mirror, me).start()

                @pl.when(inner == 1)
                def _():
                    sum_copy(phase, chunk, opposite, me).start()

                sum_copy(phase, chunk, near, me).start()
            else:
                lax.fori_loop(1, group, send, 0)
        if group == 4:

            @pl.when(inner == 1)
            def _():
                for chunk in range(CHUNKS):
                    part = slice(chunk * cols, (chunk + 1) * cols)
                    relay_copy(phase, chunk).wait_recv()
                    term = summed[phase, mirror, :, part].astype(F32)
                    term += relayed[phase, :, part].astype(F32)
                    summed[phase, mirror, :, part] = term.astype(BF16)
                    sum_copy(phase, chunk, mirror, me).start()

        between()
        for chunk in range(CHUNKS):
            part = slice(chunk * cols, (chunk + 1) * cols)
            total[:, part] += summed[phase, me, :, part].astype(F32)

            def add(step, _):
                source = peer(group - step)
                sum_copy(phase, chunk, me, source).wait_recv()
                total[:, part] += arrived[phase, source, :, part].astype(F32)
                return 0

            def add_from(source):
                sum_copy(phase, chunk, me, source).wait_recv()
                total[:, part] += arrived[phase, source, :, part].astype(F32)

            if group == 4:
                add_from(near)
                add_from(mirror)

                @pl.when(inner == 0)
                def _():
                    add_from(opposite)
            else:
                lax.fori_loop(1, group, add, 0)

    def project(phase):
        def work(slot):
            qkv[slot] = lax.dot_general(
                gathered[phase, slot],
                w_qkv[...],
                (((1,), (1,)), ((), ())),
                preferred_element_type=F32,
            ).astype(BF16)

        return work

    def expand(phase):
        def work(slot):
            row_block = gathered[phase, slot]
            gate = jnp.dot(row_block, w_gu[:, 0].reshape(width, ff), preferred_element_type=F32)
            up = jnp.dot(row_block, w_gu[:, 1].reshape(width, ff), preferred_element_type=F32)
            hidden[slot] = (gate / (1.0 + jnp.exp(-gate)) * up).astype(BF16)

        return work

    def swap_copy(phase, source):
        return pltpu.make_async_remote_copy(
            src_ref=given.at[phase, source],
            dst_ref=taken.at[phase, source],
            send_sem=e_send.at[phase, source],
            recv_sem=e_recv.at[phase, source],
            device_id=partner,
            device_id_type=MESH,
        )

    def whole_copy(phase, target, source):
        return pltpu.make_async_remote_copy(
            src_ref=summed.at[phase, target],
            dst_ref=arrived.at[phase, source],
            send_sem=r_send.at[phase, 0, target],
            recv_sem=r_recv.at[phase, 0, source],
            device_id=(place, target),
            device_id_type=MESH,
        )

    def feed(phase, values):
        work = expand(phase)
        announce(phase, values)
        work(base + me)
        if phase == 1:
            loads[7].wait()

        def give(source):
            slot = other_base + source
            block_copy(phase, slot, ag_send.at[phase, me], partner).wait_recv()
            work(slot)
            term = jnp.dot(hidden[slot], w_down[...], preferred_element_type=F32)
            given[phase, source] = term.astype(BF16)
            swap_copy(phase, source).start()

        def take(source):
            term = jnp.dot(hidden[base + source], w_down[...], preferred_element_type=F32)
            swap_copy(phase, source).wait_recv()
            return term + taken[phase, source].astype(F32)

        def give_back(source):
            summed[phase, source] = take(source).astype(BF16)
            whole_copy(phase, source, me).start()

        give(me)
        for step in range(1, 4):
            pass_on(phase, order[step - 1], step)
            work(base + order[step - 1])
            if step > 1:
                give_back(order[step - 2])
            give(order[step - 1])
        give_back(order[2])
        total[...] += take(me)
        for source in order:
            whole_copy(phase, me, source).wait_recv()
            total[...] += arrived[phase, source].astype(F32)

    def attend(memory_ref, totals_ref):
        all_rows = flat(qkv[...])
        seg = all_rows.shape[0]
        queries = all_rows[:, :head]
        keys = all_rows[:, head : 2 * head]
        values = all_rows[:, 2 * head :]
        scores = lax.dot_general(
            queries, keys, (((1,), (1,)), ((), ())), preferred_element_type=F32
        ) * head ** (-0.5)
        at_row = lax.broadcasted_iota(jnp.int32, (seg, seg), 0)
        at_col = lax.broadcasted_iota(jnp.int32, (seg, seg), 1)
        scores = jnp.where(at_row >= at_col, scores, -jnp.inf)
        powers = jnp.exp(scores - jnp.max(scores, axis=-1, keepdims=True))
        probs = (powers / jnp.sum(powers, axis=-1, keepdims=True)).astype(BF16)
        direct = jnp.dot(probs, values, preferred_element_type=F32)
        lifted_q = lifted(queries.astype(F32))
        numer = jnp.dot(
            lifted_q, memory_ref[...], preferred_element_type=F32, precision=lax.Precision.HIGHEST
        )
        denom = jnp.sum(lifted_q * totals_ref[...], axis=-1, keepdims=True)
        opened = 1.0 / (1.0 + jnp.exp(-logit[...]))
        mixed = opened * (numer / denom) + (1.0 - opened) * direct
        blended[...] = mixed.reshape(blended.shape).astype(BF16)

    def remember(memory_ref, totals_ref):
        all_rows = flat(qkv[...])
        lifted_k = lifted(all_rows[:, head : 2 * head].astype(F32))
        values = all_rows[:, 2 * head :].astype(F32)
        memory_out[...] = memory_ref[...] + lax.dot_general(
            lifted_k,
            values,
            (((0,), (0,)), ((), ())),
            preferred_element_type=F32,
            precision=lax.Precision.HIGHEST,
        )
        totals_out[...] = totals_ref[...] + jnp.sum(lifted_k, axis=0, keepdims=True)

    def layer(turn, memory_ref, totals_ref):
        first, second = 2 * turn, 2 * turn + 1
        start = stream[...].astype(F32)
        gather(first, norm(start, gain_first[pl.ds(depth, 1), :]), project(first))
        total[...] = start
        if turn == 0:
            loads[3].wait()
        attend(memory_ref, totals_ref)
        if turn == 0:
            loads[4].wait()
            loads[5].wait()
        reduce(first, blended, w_out, lambda: remember(memory_ref, totals_ref))
        middle = total[...].astype(BF16).astype(F32)
        gather_two = norm(middle, gain_second[pl.ds(depth, 1), :])
        total[...] = middle
        if group == 4:
            feed(second, gather_two)
        else:
            gather(second, gather_two, expand(second))
            if turn == 0:
                loads[7].wait()
            reduce(second, hidden, w_down, lambda: None)

    loads[0].wait()
    loads[1].wait()
    stream[...] = acts[...]
    layer(0, memory, totals)
    first_out[...] = total[...].astype(BF16)
    relay = pltpu.make_async_remote_copy(
        src_ref=first_out,
        dst_ref=shifted,
        send_sem=sh_sem.at[0],
        recv_sem=sh_sem.at[1],
        device_id=following,
        device_id_type=MESH,
    )
    relay.start()
    loads[8].wait()
    relay.wait_recv()
    stream[...] = jnp.where(depth == 0, fresh[...].astype(F32), shifted[...].astype(F32)).astype(BF16)
    layer(1, memory_out, totals_out)
    second_out[...] = total[...].astype(BF16)

    relay.wait_send()
    for phase in range(4):
        block_copy(phase, base + me, ag_send.at[phase, me], partner).wait_send()
        piped = group == 4 and phase % 2 == 1
        if piped:
            swap_copy(phase, me).wait_send()
        else:
            for chunk in range(CHUNKS):
                exchange_copy(phase, chunk).wait_send()

        def drain(step, _):
            target = peer(step)
            block_copy(phase, base + me, ag_send.at[phase, target], partner).wait_send()
            block_copy(phase, base + target, fw_send.at[phase, target], partner).wait_send()
            if piped:
                swap_copy(phase, target).wait_send()
                whole_copy(phase, target, me).wait_send()
            else:
                for chunk in range(CHUNKS):
                    sum_copy(phase, chunk, target, me).wait_send()
            return 0

        lax.fori_loop(1, group, drain, 0)


def deliver(*refs):
    sources, targets, sems = refs[:4], refs[4:8], refs[8]
    copies = [
        pltpu.make_async_copy(source, target, sems.at[k])
        for k, (source, target) in enumerate(zip(sources, targets))
    ]
    for copy in copies:
        copy.start()
    for copy in copies:
        copy.wait()


def relaid(weight):
    width, two, ff = weight.shape
    block = 256
    same = lax.broadcasted_iota(jnp.int32, (block, block), 0) == lax.broadcasted_iota(
        jnp.int32, (block, block), 1
    )
    cut = weight.reshape(width // block, block, two, ff)
    return jnp.einsum("bdtf,de->btef", cut, same.astype(BF16), preferred_element_type=BF16)


def solution(mesh):
    n_layer, group = mesh.shape["layer"], mesh.shape["tp"]

    def body(acts, fresh, g_one, g_two, p_qkv, p_out, p_gu, p_down, memory, totals, logits):
        rows, width = acts.shape
        head = memory.shape[-1]
        ff = p_down.shape[0]
        blocks = 2 * group
        gate_up = relaid(p_gu)
        vmem = pl.BlockSpec(memory_space=pltpu.VMEM)
        hbm = pl.BlockSpec(memory_space=pl.ANY)
        dma = pltpu.SemaphoreType.DMA
        outs = pl.pallas_call(
            functools.partial(kernel, n_layer, group),
            out_shape=(
                jax.ShapeDtypeStruct((rows, width), BF16),
                jax.ShapeDtypeStruct((rows, width), BF16),
                jax.ShapeDtypeStruct((head, head), F32),
                jax.ShapeDtypeStruct((1, head), F32),
            ),
            in_specs=[hbm] * 9 + [vmem] * 2,
            out_specs=(vmem,) * 4,
            scratch_shapes=[
                pltpu.VMEM((rows, width), BF16),
                pltpu.VMEM((rows, width), BF16),
                pltpu.VMEM(g_one.shape, F32),
                pltpu.VMEM(g_two.shape, F32),
                pltpu.VMEM((3 * head, width), BF16),
                pltpu.VMEM((head, width), BF16),
                pltpu.VMEM(gate_up.shape, BF16),
                pltpu.VMEM((ff, width), BF16),
                pltpu.VMEM((head, head), F32),
                pltpu.VMEM((4, blocks, rows, width), BF16),
                pltpu.VMEM((blocks, rows, 3 * head), BF16),
                pltpu.VMEM((blocks, rows, head), BF16),
                pltpu.VMEM((blocks, rows, ff), BF16),
                pltpu.VMEM((4, group, rows, width), BF16),
                pltpu.VMEM((4, group, rows, width), BF16),
                pltpu.VMEM((4, group, rows, width), BF16),
                pltpu.VMEM((4, group, rows, width), BF16),
                pltpu.VMEM((4, rows, width), BF16),
                pltpu.VMEM((rows, width), BF16),
                pltpu.VMEM((rows, width), F32),
                pltpu.VMEM((rows, width), BF16),
                dma((9,)),
                dma((4, group)),
                dma((4, group)),
                dma((4, blocks)),
                dma((4, CHUNKS)),
                dma((4, CHUNKS)),
                dma((4, CHUNKS, group)),
                dma((4, CHUNKS, group)),
                dma((4, CHUNKS)),
                dma((4, group)),
                dma((4, group)),
                dma((2,)),
            ],
            compiler_params=pltpu.CompilerParams(
                collective_id=0, has_side_effects=True, vmem_limit_bytes=58 * 1024 * 1024
            ),
        )(
            acts,
            fresh,
            g_one,
            g_two,
            jnp.swapaxes(p_qkv[0], 0, 1),
            p_out,
            gate_up,
            p_down,
            memory[0],
            totals,
            logits[:, None],
        )
        first, second, after, norms = pl.pallas_call(
            deliver,
            out_shape=[jax.ShapeDtypeStruct(o.shape, o.dtype) for o in outs],
            in_specs=[vmem] * 4,
            out_specs=[hbm] * 4,
            scratch_shapes=[dma((4,))],
        )(*outs)
        return first, second, after[None], norms

    both = ("layer", "tp")
    in_specs = (
        P(both, None),
        P(None, "tp", None),
        P(),
        P(),
        P(both, None, None),
        P(both, None),
        P(None, None, both),
        P(both, None),
        P(both, None, None),
        P(both, None),
        P(both),
    )
    out_specs = (P(both, None), P(both, None), P(both, None, None), P(both, None))
    return jax.shard_map(body, mesh=mesh, in_specs=in_specs, out_specs=out_specs, check_vma=False)
```
